32 devices in a mesh: scene: 2 (over x), row: 16 (over z, y, core).
Axes of the slice: x: 2, y: 2, z: 4, core: 2. Of those that a mesh axis runs over, the one named last changes fastest.
Arguments:
- echoes: bfloat16 [2048, 2, 8192], P(('scene', 'row')), parts along dimension 0, may hold values from -6 to 6
- range_replica: bfloat16 [2, 1024], replicated, may hold values from -0.125 to 0.125
- azimuth_replicas: bfloat16 [16, 2, 512], replicated, may hold values from -0.1875 to 0.1875
- replica_index: int32 [16384], P(('scene', 'row')), parts along dimension 0, may hold values from 0 to 15
- azimuth_extent: int32 [128], P('scene'), parts along dimension 0, may hold values from 0 to 16
- range_extent: int32 [1024], P('scene'), parts along dimension 0, may hold values from 0 to 16
Outputs:
- focused: bfloat16 [2048, 2, 8192], P('scene', None, 'row'), parts along dimension 0
- looked: float32 [1024, 64], P(('scene', 'row')), parts along dimension 0
The draws below stay inside these ranges and needn't reach their ends.
There are 2 independent parts, one for each index of `scene`. The reference program is written for one: setup_inputs(seed, part) draws one part's arguments, and reference() takes and returns one part's arrays. A program takes and returns all parts, laid end to end along the dimension named above; an argument that names none is the same for every part. Nothing has to cross between parts.
All inputs are finite; a program needn't handle non-finite values.
Results may differ from the reference program's by a relative error of at most 0.0049.
Values may be sent and summed in bfloat16 or wider, within the bound.
A program may use at most 128 MiB of HBM per device.

```python
import jax
import jax.numpy as jnp
from jax import lax

P_SIZE = 1024
S = 8192
K_RG = 1024
K_AZ = 512
NF = 16
TILE = 16
EXT = 16


def extent_values(key, count, salt):
    base_key = jax.random.fold_in(key, salt)
    values = jax.random.randint(jax.random.fold_in(base_key, 1), (count,), 0, EXT + 1, dtype=jnp.int32)
    spots = jax.random.permutation(jax.random.fold_in(base_key, 2), count)
    return values.at[spots[0]].set(EXT).at[spots[1]].set(0)


def draw_azimuth_extent(key, part):
    return extent_values(key, P_SIZE // TILE, 7)


def draw_range_extent(key, part):
    return extent_values(key, S // TILE, 9)


def with_ends(values, stream_key, smallest, largest):
    longest = values.shape.index(max(values.shape))
    spots = []
    for shift in (0, 1):
        where = [jax.random.randint(jax.random.fold_in(stream_key, axis), (), 0, length) for axis, length in enumerate(values.shape)]
        where[longest] = (where[longest] + shift) % values.shape[longest]
        spots.append(tuple(where))
    return values.at[spots[0]].set(smallest).at[spots[1]].set(largest)


def block_levels(own_key, shape, shards, smallest, top_value):
    loudness = 1.0
    for position, blocks in shards:
        heights = jax.random.uniform(jax.random.fold_in(jax.random.fold_in(own_key, 6), position), (blocks,), jnp.float32, smallest / len(shards), top_value / len(shards))
        loudness = loudness * jnp.repeat(jnp.exp(heights), shape[position] // blocks).reshape((-1,) + (1,) * (len(shape) - 1 - position))
    return loudness


def gaussian(own_key, shape, spread, bound, shards=(), kind=jnp.bfloat16):
    drawn = spread * jax.random.normal(own_key, shape, jnp.float32)
    if shards:
        drawn = drawn * block_levels(own_key, shape, shards, -0.22, 0.18)
    return jnp.clip(drawn, -bound, bound).astype(kind)


def setup_inputs(seed: int = 0, part: int = 0) -> dict:
    arg_keys = jax.random.split(jax.random.key(seed), 7)
    part_keys = jax.random.split(jax.random.fold_in(arg_keys[6], part), 7)
    return {
        "echoes": gaussian(part_keys[0], (P_SIZE, 2, S), 1.0, 6.0, ((0, 16),)),
        "range_replica": gaussian(arg_keys[1], (2, K_RG), (2 * K_RG) ** -0.5, 0.125),
        "azimuth_replicas": gaussian(arg_keys[2], (NF, 2, K_AZ), (2 * K_AZ) ** -0.5, 0.1875),
        "replica_index": with_ends(jax.random.randint(part_keys[3], (S,), 0, NF), jax.random.fold_in(part_keys[3], 1), 0, NF - 1).astype(jnp.int32),
        "azimuth_extent": draw_azimuth_extent(jax.random.fold_in(jax.random.fold_in(arg_keys[6], part), 71), part),
        "range_extent": draw_range_extent(jax.random.fold_in(jax.random.fold_in(arg_keys[6], part), 71), part),
    }


HIGHEST = lax.Precision.HIGHEST


def window_mask(count_tiles, count_cells, extent):
    cells = jnp.arange(count_cells, dtype=jnp.int32)
    starts = jnp.arange(count_tiles, dtype=jnp.int32) * TILE - extent
    stops = starts + TILE + 2 * extent
    inside = (cells[None, :] >= starts[:, None]) & (cells[None, :] < stops[:, None])
    return inside.astype(jnp.float32)


def reference(echoes, range_replica, azimuth_replicas, replica_index, azimuth_extent, range_extent):
    pulses = echoes.shape[0]
    samples = echoes.shape[2]
    tap_count = range_replica.shape[1]
    padded_length = samples + tap_count
    signal = lax.complex(echoes[:, 0, :].astype(jnp.float32), echoes[:, 1, :].astype(jnp.float32))
    kernel = lax.complex(range_replica[0].astype(jnp.float32), range_replica[1].astype(jnp.float32))
    signal_spectrum = jnp.fft.fft(signal, n=padded_length, axis=1)
    kernel_spectrum = jnp.fft.fft(kernel, n=padded_length)
    compressed_full = jnp.fft.ifft(signal_spectrum * jnp.conj(kernel_spectrum)[None, :], axis=1)[:, :samples]
    comp_real = jnp.real(compressed_full).astype(jnp.bfloat16)
    comp_imag = jnp.imag(compressed_full).astype(jnp.bfloat16)
    comp_real, comp_imag = lax.optimization_barrier((comp_real, comp_imag))
    turned = lax.complex(comp_real.astype(jnp.float32), comp_imag.astype(jnp.float32))
    turned_spectrum = jnp.fft.fft(turned, axis=0)
    replicas = lax.complex(azimuth_replicas[:, 0, :].astype(jnp.float32), azimuth_replicas[:, 1, :].astype(jnp.float32))
    replica_spectra = jnp.fft.fft(replicas, n=pulses, axis=1)
    chosen = jnp.take(replica_spectra.T, replica_index, axis=1)
    azimuth = jnp.fft.ifft(turned_spectrum * jnp.conj(chosen), axis=0)
    az_real = jnp.real(azimuth)
    az_imag = jnp.imag(azimuth)
    focused = jnp.stack([az_real, az_imag], axis=1).astype(jnp.bfloat16)
    intensity = az_real * az_real + az_imag * az_imag
    pulse_mask = window_mask(pulses // TILE, pulses, azimuth_extent)
    range_mask = window_mask(samples // TILE, samples, range_extent)
    row_sums = jnp.dot(pulse_mask, intensity, precision=HIGHEST, preferred_element_type=jnp.float32)
    window_sums = jnp.dot(range_mask, row_sums.T, precision=HIGHEST, preferred_element_type=jnp.float32)
    counts = jnp.sum(range_mask, axis=1)[:, None] * jnp.sum(pulse_mask, axis=1)[None, :]
    looked = window_sums / counts
    return focused, looked
```

```python
import functools

import jax
import jax.numpy as jnp
import numpy as np
from jax import lax
from jax.experimental import pallas as pl
from jax.experimental.pallas import tpu as pltpu
from jax.sharding import PartitionSpec as P

TILE = 16
EXT = 16
CHUNKS = 2
HIGHEST = lax.Precision.HIGHEST
BF = jnp.bfloat16
F32 = jnp.float32


def mxu(left, right):
    return jnp.dot(left, right, preferred_element_type=F32)


def toeplitz_kernel(width, taps_ref, out_ref):
    for part in range(2):
        taps = jnp.broadcast_to(taps_ref[part : part + 1, :], (width, taps_ref.shape[1]))
        band = pltpu.roll(taps, 0, 1, stride=1, stride_axis=0)
        out_ref[:, part * width : (part + 1) * width] = band.T.astype(BF)


def toeplitz(range_replica, width):
    depth = range_replica.shape[1] + width
    taps = jnp.pad(range_replica.astype(F32), ((0, 0), (0, width)))
    return pl.pallas_call(
        functools.partial(toeplitz_kernel, width),
        out_shape=jax.ShapeDtypeStruct((depth, 2 * width), BF),
        name="toeplitz",
    )(taps)


def compress_kernel(group, bins, start, width, x_ref, t_ref, out_ref):
    step = pl.program_id(0)
    depth = t_ref.shape[0]
    rows = x_ref.shape[0]
    half = rows // 2
    windows = []
    for i in range(group):
        offset = pl.multiple_of((step * group + i) * bins + start, 128)
        windows.append(x_ref[:, pl.ds(offset, depth)])
    result = mxu(jnp.concatenate(windows, axis=0), t_ref[...])
    result = result.reshape(group, rows, 2 * width)
    out_ref[:, :half, :] = (result[:, :half, :width] + result[:, half:, width:]).astype(BF)
    out_ref[:, half:, :] = (result[:, half:, :width] - result[:, :half, width:]).astype(BF)


def compress(x, bands, devices, bins, start, width):
    rows = x.shape[0]
    group = max(1, min(devices, 1024 // rows))
    depth = bands.shape[0]
    return pl.pallas_call(
        functools.partial(compress_kernel, group, bins, start, width),
        grid=(devices // group,),
        in_specs=[
            pl.BlockSpec(x.shape, lambda g: (0, 0)),
            pl.BlockSpec(bands.shape, lambda g: (0, 0)),
        ],
        out_specs=pl.BlockSpec((group, rows, width), lambda g: (g, 0, 0)),
        out_shape=jax.ShapeDtypeStruct((devices, rows, width), BF),
        compiler_params=pltpu.CompilerParams(vmem_limit_bytes=48 * 2**20),
        cost_estimate=pl.CostEstimate(
            flops=2 * devices * rows * depth * 2 * width,
            bytes_accessed=4 * devices * rows * width,
            transcendentals=0,
        ),
        name="compress",
    )(x, bands)


def spectra_kernel(c_ref, s_ref, g_ref, out_ref):
    taps = g_ref.shape[1]
    gr, gi = g_ref[0], g_ref[1]
    c, s = c_ref[:, :taps], s_ref[:, :taps]
    real = mxu(c, gr) + mxu(s, gi)
    imag = mxu(c, gi) - mxu(s, gr)
    for part, value in enumerate((real, imag)):
        high = value.astype(BF)
        low = (value - high.astype(F32)).astype(BF)
        out_ref[part] = jnp.concatenate([high, low], axis=1)


def azimuth_kernel(c_ref, s_ref, y_ref, g_ref, index_ref, mask_ref, out_ref, sums_ref):
    devices, rows, width = y_ref.shape
    half = rows // 2
    pulses = devices * half
    c, s = c_ref[...], s_ref[...]
    yr = y_ref[:, :half, :].reshape(pulses, width)
    yi = y_ref[:, half:, :].reshape(pulses, width)
    fr = mxu(c, yr) + mxu(s, yi)
    fi = mxu(c, yi) - mxu(s, yr)
    replicas = g_ref.shape[2] // 2
    which = lax.rem(lax.broadcasted_iota(jnp.int32, (2 * replicas, width), 0), replicas)
    pick = (which == index_ref[...]).astype(BF)
    gr = mxu(g_ref[0], pick)
    gi = mxu(g_ref[1], pick)
    scale = 1.0 / pulses
    zr = ((fr * gr + fi * gi) * scale).astype(BF)
    zi = ((fi * gr - fr * gi) * scale).astype(BF)
    ar = mxu(c, zr) - mxu(s, zi)
    ai = mxu(c, zi) + mxu(s, zr)
    out_ref[0] = ar.astype(BF)
    out_ref[1] = ai.astype(BF)
    power = ar * ar + ai * ai
    high = power.astype(BF)
    low = (power - high.astype(F32)).astype(BF)
    mask = mask_ref[...]
    sums_ref[...] = mxu(mask, high) + mxu(mask, low)


def azimuth(cos, sin, y, spectra, index, mask):
    pulses, width = cos.shape[0], y.shape[2]
    return pl.pallas_call(
        azimuth_kernel,
        out_shape=(
            jax.ShapeDtypeStruct((2, pulses, width), BF),
            jax.ShapeDtypeStruct((mask.shape[0], width), F32),
        ),
        compiler_params=pltpu.CompilerParams(vmem_limit_bytes=56 * 2**20),
        cost_estimate=pl.CostEstimate(
            flops=16 * pulses * pulses * width,
            bytes_accessed=4 * pulses * pulses + 8 * pulses * width,
            transcendentals=0,
        ),
        name="azimuth",
    )(cos, sin, y, spectra, index, mask)


def dft_tables(length):
    steps = np.arange(length, dtype=np.int64)
    angles = (np.outer(steps, steps) % length) * (2.0 * np.pi / length)
    return jnp.asarray(np.cos(angles), dtype=BF), jnp.asarray(np.sin(angles), dtype=BF)


def window_columns(positions, starts, stops):
    inside = (positions[:, None] >= starts[None, :]) & (positions[:, None] < stops[None, :])
    return inside.astype(F32)


def per_device(
    echoes, range_replica, azimuth_replicas, replica_index, azimuth_extent, range_extent
):
    devices = lax.axis_size("row")
    local_pulses, _, samples = echoes.shape
    taps = range_replica.shape[1]
    pulses = local_pulses * devices
    range_bins = samples // devices
    chunks = CHUNKS if range_bins % (128 * CHUNKS) == 0 else 1
    width = range_bins // chunks

    bands = toeplitz(range_replica, width)
    rows = echoes.transpose(1, 0, 2).reshape(2 * local_pulses, samples)
    rows = jnp.pad(rows, ((0, 0), (0, taps)))
    cos, sin = dft_tables(pulses)
    spectra = pl.pallas_call(
        spectra_kernel,
        out_shape=jax.ShapeDtypeStruct((2, pulses, 2 * azimuth_replicas.shape[0]), BF),
        compiler_params=pltpu.CompilerParams(vmem_limit_bytes=48 * 2**20),
        name="spectra",
    )(cos, sin, azimuth_replicas.transpose(1, 2, 0))

    tile_rows = pulses // TILE
    pulse_start = jnp.arange(tile_rows, dtype=jnp.int32) * TILE - azimuth_extent
    pulse_stop = pulse_start + TILE + 2 * azimuth_extent
    pulse_mask = window_columns(jnp.arange(pulses, dtype=jnp.int32), pulse_start, pulse_stop).T
    pulse_count = (jnp.minimum(pulse_stop, pulses) - jnp.maximum(pulse_start, 0)).astype(F32)
    pulse_mask = pulse_mask.astype(BF)

    images, sums = [], []
    for q in range(chunks):
        packed = compress(rows, bands, devices, range_bins, q * width, width)
        turned = lax.all_to_all(packed, "row", split_axis=0, concat_axis=0, tiled=True)
        index = replica_index[q * width : (q + 1) * width].reshape(1, width)
        image, row_sum = azimuth(cos, sin, turned, spectra, index, pulse_mask)
        images.append(image)
        sums.append(row_sum)
    focused = jnp.concatenate(images, axis=2).transpose(1, 0, 2)
    ends = devices - 1
    before = lax.ppermute(sums[-1][:, width - EXT :], "row", [(i, i + 1) for i in range(ends)])
    after = lax.ppermute(sums[0][:, :EXT], "row", [(i + 1, i) for i in range(ends)])
    row_sums = jnp.concatenate([before, *sums, after], axis=1)

    local_tiles = range_bins // TILE
    device = lax.axis_index("row")
    tile_ids = device * local_tiles + jnp.arange(local_tiles, dtype=jnp.int32)
    local_extent = lax.dynamic_slice_in_dim(range_extent, device * local_tiles, local_tiles)
    range_start = tile_ids * TILE - local_extent
    range_stop = range_start + TILE + 2 * local_extent
    range_count = (
        jnp.minimum(range_stop, samples) - jnp.maximum(range_start, 0)
    ).astype(F32)
    positions = device * range_bins - EXT + jnp.arange(range_bins + 2 * EXT, dtype=jnp.int32)
    range_mask = window_columns(positions, range_start, range_stop)
    window_sums = jnp.einsum(
        "ct,ic->ti", range_mask, row_sums, precision=HIGHEST, preferred_element_type=F32
    )
    looked = window_sums / (range_count[:, None] * pulse_count[None, :])
    return (focused, looked)


def solution(mesh):
    return jax.shard_map(
        per_device,
        mesh=mesh,
        in_specs=(
            P(("scene", "row"), None, None),
            P(),
            P(),
            P(("scene", "row")),
            P("scene"),
            P("scene"),
        ),
        out_specs=(P("scene", None, "row"), P(("scene", "row"), None)),
        check_vma=False,
    )
```

```python
import functools

import jax
import jax.numpy as jnp
import numpy as np
from jax import lax
from jax.experimental import pallas as pl
from jax.experimental.pallas import tpu as pltpu
from jax.sharding import PartitionSpec as P

TILE = 16
EXT = 16
HIGHEST = lax.Precision.HIGHEST
BF = jnp.bfloat16
F32 = jnp.float32


def mxu(left, right):
    return jnp.dot(left, right, preferred_element_type=F32)


def toeplitz_kernel(width, taps_ref, out_ref):
    for part in range(2):
        taps = jnp.broadcast_to(taps_ref[part : part + 1, :], (width, taps_ref.shape[1]))
        band = pltpu.roll(taps, 0, 1, stride=1, stride_axis=0)
        out_ref[:, part * width : (part + 1) * width] = band.T.astype(BF)


def toeplitz(range_replica, width):
    depth = range_replica.shape[1] + width
    taps = jnp.pad(range_replica.astype(F32), ((0, 0), (0, width)))
    return pl.pallas_call(
        functools.partial(toeplitz_kernel, width),
        out_shape=jax.ShapeDtypeStruct((depth, 2 * width), BF),
        name="toeplitz",
    )(taps)


def block(x_ref, t_ref, offsets):
    rows = x_ref.shape[0]
    half = rows // 2
    depth = t_ref.shape[0]
    width = t_ref.shape[1] // 2
    windows = [x_ref[:, pl.ds(offset, depth)] for offset in offsets]
    result = mxu(jnp.concatenate(windows, axis=0), t_ref[...])
    result = result.reshape(len(offsets), rows, 2 * width)
    real = result[:, :half, :width] + result[:, half:, width:]
    imag = result[:, half:, :width] - result[:, :half, width:]
    return jnp.concatenate([real, imag], axis=1).astype(BF)


def compress_kernel(group, bins, x_ref, t_ref, out_ref):
    step = pl.program_id(0)
    width = t_ref.shape[1] // 2
    for start in range(0, bins, width):
        offsets = [
            pl.multiple_of((step * group + i) * bins + start, 128) for i in range(group)
        ]
        out_ref[:, :, start : start + width] = block(x_ref, t_ref, offsets)


def exchange(x, bands, devices, bins):
    rows = x.shape[0]
    group = max(1, min(devices, 1024 // rows))
    packed = pl.pallas_call(
        functools.partial(compress_kernel, group, bins),
        grid=(devices // group,),
        in_specs=[
            pl.BlockSpec(x.shape, lambda g: (0, 0)),
            pl.BlockSpec(bands.shape, lambda g: (0, 0)),
        ],
        out_specs=pl.BlockSpec((group, rows, bins), lambda g: (g, 0, 0)),
        out_shape=jax.ShapeDtypeStruct((devices, rows, bins), BF),
        compiler_params=pltpu.CompilerParams(vmem_limit_bytes=48 * 2**20),
        name="compress",
    )(x, bands)
    return lax.all_to_all(packed, "row", split_axis=0, concat_axis=0, tiled=True)


def butterfly(parts, sign):
    radix = len(parts)
    if radix == 1:
        return parts
    (ar, ai), (br, bi), (cr, ci), (dr, di) = parts
    pr, pi, qr, qi = ar + cr, ai + ci, ar - cr, ai - ci
    tr, ti, ur, ui = br + dr, bi + di, br - dr, bi - di
    return [
        (pr + tr, pi + ti),
        (qr - sign * ui, qi + sign * ur),
        (pr - tr, pi - ti),
        (qr + sign * ui, qi - sign * ur),
    ]


def forward(table_ref, subsets, length):
    parts = []
    for j, (yr, yi) in enumerate(subsets):
        c, s = table_ref[j, 0, :, :length], table_ref[j, 1, :, :length]
        parts.append((mxu(c, yr) + mxu(s, yi), mxu(c, yi) - mxu(s, yr)))
    return butterfly(parts, -1.0)


def spectra_kernel(table_ref, g_ref, out_ref):
    radix, length = g_ref.shape[1], g_ref.shape[2]
    subsets = [(g_ref[0, j], g_ref[1, j]) for j in range(radix)]
    for m, pair in enumerate(forward(table_ref, subsets, length)):
        for part, value in enumerate(pair):
            high = value.astype(BF)
            low = (value - high.astype(F32)).astype(BF)
            out_ref[part, m] = jnp.concatenate([high, low], axis=1)


def azimuth_kernel(table_ref, back_ref, y_ref, g_ref, index_ref, mask_ref, out_ref, sums_ref):
    devices, rows, width = y_ref.shape
    radix, _, quarter, _ = table_ref.shape
    piece = rows // (2 * radix)

    def subset(k):
        return y_ref[:, k * piece : (k + 1) * piece, :].reshape(quarter, width)

    spectrum = forward(table_ref, [(subset(j), subset(radix + j)) for j in range(radix)], quarter)
    replicas = g_ref.shape[3] // 2
    which = lax.rem(lax.broadcasted_iota(jnp.int32, (2 * replicas, width), 0), replicas)
    pick = (which == index_ref[...]).astype(BF)
    scale = 1.0 / (radix * quarter)
    product = []
    for m, (fr, fi) in enumerate(spectrum):
        gr = mxu(g_ref[0, m], pick) * scale
        gi = mxu(g_ref[1, m], pick) * scale
        product.append((fr * gr + fi * gi, fi * gr - fr * gi))
    sums = jnp.zeros(sums_ref.shape, F32)
    for j, (zr, zi) in enumerate(butterfly(product, 1.0)):
        zr, zi = zr.astype(BF), zi.astype(BF)
        c, s = back_ref[j, 0], back_ref[j, 1]
        ar = mxu(c, zr) - mxu(s, zi)
        ai = mxu(c, zi) + mxu(s, zr)
        out_ref[0, j] = ar.astype(BF)
        out_ref[1, j] = ai.astype(BF)
        power = ar * ar + ai * ai
        high = power.astype(BF)
        low = (power - high.astype(F32)).astype(BF)
        mask = mask_ref[j]
        sums = sums + mxu(mask, high) + mxu(mask, low)
    sums_ref[...] = sums


def azimuth(table, back, y, spectra, index, mask, width):
    devices, rows, bins = y.shape
    radix, _, quarter, _ = table.shape
    return pl.pallas_call(
        azimuth_kernel,
        grid=(bins // width,),
        in_specs=[
            pl.BlockSpec(table.shape, lambda c: (0, 0, 0, 0)),
            pl.BlockSpec(back.shape, lambda c: (0, 0, 0, 0)),
            pl.BlockSpec((devices, rows, width), lambda c: (0, 0, c)),
            pl.BlockSpec(spectra.shape, lambda c: (0, 0, 0, 0)),
            pl.BlockSpec((1, width), lambda c: (0, c)),
            pl.BlockSpec(mask.shape, lambda c: (0, 0, 0)),
        ],
        out_specs=(
            pl.BlockSpec((2, radix, quarter, width), lambda c: (0, 0, 0, c)),
            pl.BlockSpec((mask.shape[1], width), lambda c: (0, c)),
        ),
        out_shape=(
            jax.ShapeDtypeStruct((2, radix, quarter, bins), BF),
            jax.ShapeDtypeStruct((mask.shape[1], bins), F32),
        ),
        compiler_params=pltpu.CompilerParams(vmem_limit_bytes=48 * 2**20),
        name="azimuth",
    )(table, back, y, spectra, index, mask)


def dft_tables(length, radix):
    quarter = length // radix
    freq = np.arange(quarter, dtype=np.int64)
    tables = []
    for j in range(radix):
        pulse = radix * np.arange(quarter, dtype=np.int64) + j
        angles = (np.outer(freq, pulse) % length) * (2.0 * np.pi / length)
        tables.append(np.stack([np.cos(angles), np.sin(angles)]))
    table = np.stack(tables)
    return jnp.asarray(table, dtype=BF), jnp.asarray(table.swapaxes(2, 3), dtype=BF)


def window_columns(positions, starts, stops):
    inside = (positions[:, None] >= starts[None, :]) & (positions[:, None] < stops[None, :])
    return inside.astype(F32)


def per_device(
    echoes, range_replica, azimuth_replicas, replica_index, azimuth_extent, range_extent
):
    devices = lax.axis_size("row")
    local_pulses, _, samples = echoes.shape
    taps = range_replica.shape[1]
    pulses = local_pulses * devices
    range_bins = samples // devices
    width = 256 if range_bins % 256 == 0 else 128
    radix = 4 if local_pulses % 64 == 0 else 1
    quarter = pulses // radix

    bands = toeplitz(range_replica, width)
    rows = echoes.reshape(local_pulses // radix, radix, 2, samples).transpose(2, 1, 0, 3)
    rows = jnp.pad(rows.reshape(2 * local_pulses, samples), ((0, 0), (0, taps)))
    table, back = dft_tables(pulses, radix)
    replicas, _, azimuth_taps = azimuth_replicas.shape
    split = azimuth_replicas.reshape(replicas, 2, azimuth_taps // radix, radix)
    spectra = pl.pallas_call(
        spectra_kernel,
        out_shape=jax.ShapeDtypeStruct((2, radix, quarter, 2 * replicas), BF),
        compiler_params=pltpu.CompilerParams(vmem_limit_bytes=48 * 2**20),
        name="spectra",
    )(table, split.transpose(1, 3, 2, 0))

    tile_rows = pulses // TILE
    pulse_start = jnp.arange(tile_rows, dtype=jnp.int32) * TILE - azimuth_extent
    pulse_stop = pulse_start + TILE + 2 * azimuth_extent
    order = jnp.arange(radix, dtype=jnp.int32)[:, None, None] + radix * jnp.arange(
        quarter, dtype=jnp.int32
    )
    pulse_mask = (order >= pulse_start[:, None]) & (order < pulse_stop[:, None])
    pulse_count = (jnp.minimum(pulse_stop, pulses) - jnp.maximum(pulse_start, 0)).astype(F32)
    pulse_mask = pulse_mask.astype(BF)

    turned = exchange(rows, bands, devices, range_bins)
    index = replica_index.reshape(1, range_bins)
    image, sums = azimuth(table, back, turned, spectra, index, pulse_mask, width)
    focused = image.transpose(2, 1, 0, 3).reshape(pulses, 2, range_bins)
    ends = devices - 1
    before = lax.ppermute(sums[:, range_bins - EXT :], "row", [(i, i + 1) for i in range(ends)])
    after = lax.ppermute(sums[:, :EXT], "row", [(i + 1, i) for i in range(ends)])
    row_sums = jnp.concatenate([before, sums, after], axis=1)

    local_tiles = range_bins // TILE
    device = lax.axis_index("row")
    tile_ids = device * local_tiles + jnp.arange(local_tiles, dtype=jnp.int32)
    local_extent = lax.dynamic_slice_in_dim(range_extent, device * local_tiles, local_tiles)
    range_start = tile_ids * TILE - local_extent
    range_stop = range_start + TILE + 2 * local_extent
    range_count = (
        jnp.minimum(range_stop, samples) - jnp.maximum(range_start, 0)
    ).astype(F32)
    positions = device * range_bins - EXT + jnp.arange(range_bins + 2 * EXT, dtype=jnp.int32)
    range_mask = window_columns(positions, range_start, range_stop)
    window_sums = jnp.einsum(
        "ct,ic->ti", range_mask, row_sums, precision=HIGHEST, preferred_element_type=F32
    )
    looked = window_sums / (range_count[:, None] * pulse_count[None, :])
    return (focused, looked)


def solution(mesh):
    return jax.shard_map(
        per_device,
        mesh=mesh,
        in_specs=(
            P(("scene", "row"), None, None),
            P(),
            P(),
            P(("scene", "row")),
            P("scene"),
            P("scene"),
        ),
        out_specs=(P("scene", None, "row"), P(("scene", "row"), None)),
        check_vma=False,
    )
```

```python
import functools

import jax
import jax.numpy as jnp
import numpy as np
from jax import lax
from jax.experimental import pallas as pl
from jax.experimental.pallas import tpu as pltpu
from jax.sharding import PartitionSpec as P

TILE = 16
EXT = 16
HIGHEST = lax.Precision.HIGHEST
BF = jnp.bfloat16
F32 = jnp.float32


def mxu(left, right):
    return jnp.dot(left, right, preferred_element_type=F32)


def toeplitz_kernel(width, taps_ref, out_ref):
    for part in range(2):
        taps = jnp.broadcast_to(taps_ref[part : part + 1, :], (width, taps_ref.shape[1]))
        band = pltpu.roll(taps, 0, 1, stride=1, stride_axis=0)
        out_ref[:, part * width : (part + 1) * width] = band.T.astype(BF)


def toeplitz(range_replica, width):
    depth = range_replica.shape[1] + width
    taps = jnp.pad(range_replica.astype(F32), ((0, 0), (0, width)))
    return pl.pallas_call(
        functools.partial(toeplitz_kernel, width),
        out_shape=jax.ShapeDtypeStruct((depth, 2 * width), BF),
        name="toeplitz",
    )(taps)


def block(x_ref, t_ref, offsets):
    rows = x_ref.shape[0]
    half = rows // 2
    depth = t_ref.shape[0]
    width = t_ref.shape[1] // 2
    windows = [x_ref[:, pl.ds(offset, depth)] for offset in offsets]
    result = mxu(jnp.concatenate(windows, axis=0), t_ref[...])
    result = result.reshape(len(offsets), rows, 2 * width)
    real = result[:, :half, :width] + result[:, half:, width:]
    imag = result[:, half:, :width] - result[:, :half, width:]
    return jnp.concatenate([real, imag], axis=1).astype(BF)


def exchange_kernel(devices, bins, x_ref, t_ref, out_ref, packed, send_sems, recv_sems, own_sem):
    me = lax.axis_index("row")
    width = t_ref.shape[1] // 2
    barrier = pltpu.get_barrier_semaphore()

    def greet(i, carry):
        pl.semaphore_signal(
            barrier,
            inc=1,
            device_id={"row": lax.rem(me + i, devices)},
            device_id_type=pl.DeviceIdType.MESH,
        )
        return carry

    lax.fori_loop(1, devices, greet, 0)

    def fill(target):
        for start in range(0, bins, width):
            offset = pl.multiple_of(target * bins + start, 128)
            packed[target, :, start : start + width] = block(x_ref, t_ref, [offset])[0]

    def remote(i):
        target = lax.rem(me + i, devices)
        return pltpu.make_async_remote_copy(
            src_ref=packed.at[target],
            dst_ref=out_ref.at[me],
            send_sem=send_sems.at[i],
            recv_sem=recv_sems.at[i],
            device_id={"row": target},
            device_id_type=pl.DeviceIdType.MESH,
        )

    fill(lax.rem(me + 1, devices))
    pl.semaphore_wait(barrier, devices - 1)

    def step(i, carry):
        remote(i).start()
        fill(lax.rem(me + i + 1, devices))
        return carry

    lax.fori_loop(1, devices, step, 0)
    own = pltpu.make_async_copy(packed.at[me], out_ref.at[me], own_sem)
    own.start()

    def finish(i, carry):
        remote(i).wait()
        return carry

    lax.fori_loop(1, devices, finish, 0)
    own.wait()


def exchange(x, bands, devices, bins):
    rows = x.shape[0]
    return pl.pallas_call(
        functools.partial(exchange_kernel, devices, bins),
        in_specs=[pl.BlockSpec(memory_space=pltpu.VMEM)] * 2,
        out_specs=pl.BlockSpec(memory_space=pl.ANY),
        out_shape=jax.ShapeDtypeStruct((devices, rows, bins), BF),
        scratch_shapes=[
            pltpu.VMEM((devices, rows, bins), BF),
            pltpu.SemaphoreType.DMA((devices,)),
            pltpu.SemaphoreType.DMA((devices,)),
            pltpu.SemaphoreType.DMA,
        ],
        compiler_params=pltpu.CompilerParams(
            collective_id=0, has_side_effects=True, vmem_limit_bytes=48 * 2**20
        ),
        name="exchange",
    )(x, bands)


def butterfly(parts, sign):
    radix = len(parts)
    if radix == 1:
        return parts
    (ar, ai), (br, bi), (cr, ci), (dr, di) = parts
    pr, pi, qr, qi = ar + cr, ai + ci, ar - cr, ai - ci
    tr, ti, ur, ui = br + dr, bi + di, br - dr, bi - di
    return [
        (pr + tr, pi + ti),
        (qr - sign * ui, qi + sign * ur),
        (pr - tr, pi - ti),
        (qr + sign * ui, qi - sign * ur),
    ]


def forward(table_ref, subsets, length):
    parts = []
    for j, (yr, yi) in enumerate(subsets):
        c, s = table_ref[j, 0, :, :length], table_ref[j, 1, :, :length]
        parts.append((mxu(c, yr) + mxu(s, yi), mxu(c, yi) - mxu(s, yr)))
    return butterfly(parts, -1.0)


def spectra_kernel(table_ref, g_ref, out_ref):
    radix, length = g_ref.shape[1], g_ref.shape[2]
    subsets = [(g_ref[0, j], g_ref[1, j]) for j in range(radix)]
    for m, pair in enumerate(forward(table_ref, subsets, length)):
        for part, value in enumerate(pair):
            high = value.astype(BF)
            low = (value - high.astype(F32)).astype(BF)
            out_ref[part, m] = jnp.concatenate([high, low], axis=1)


def azimuth_kernel(table_ref, back_ref, y_ref, g_ref, index_ref, mask_ref, out_ref, sums_ref):
    devices, rows, width = y_ref.shape
    radix, _, quarter, _ = table_ref.shape
    piece = rows // (2 * radix)

    def subset(k):
        return y_ref[:, k * piece : (k + 1) * piece, :].reshape(quarter, width)

    spectrum = forward(table_ref, [(subset(j), subset(radix + j)) for j in range(radix)], quarter)
    replicas = g_ref.shape[3] // 2
    which = lax.rem(lax.broadcasted_iota(jnp.int32, (2 * replicas, width), 0), replicas)
    pick = (which == index_ref[...]).astype(BF)
    scale = 1.0 / (radix * quarter)
    product = []
    for m, (fr, fi) in enumerate(spectrum):
        gr = mxu(g_ref[0, m], pick) * scale
        gi = mxu(g_ref[1, m], pick) * scale
        product.append((fr * gr + fi * gi, fi * gr - fr * gi))
    sums = jnp.zeros(sums_ref.shape, F32)
    for j, (zr, zi) in enumerate(butterfly(product, 1.0)):
        zr, zi = zr.astype(BF), zi.astype(BF)
        c, s = back_ref[j, 0], back_ref[j, 1]
        ar = mxu(c, zr) - mxu(s, zi)
        ai = mxu(c, zi) + mxu(s, zr)
        out_ref[0, j] = ar.astype(BF)
        out_ref[1, j] = ai.astype(BF)
        power = ar * ar + ai * ai
        high = power.astype(BF)
        low = (power - high.astype(F32)).astype(BF)
        mask = mask_ref[j]
        sums = sums + mxu(mask, high) + mxu(mask, low)
    sums_ref[...] = sums


def azimuth(table, back, y, spectra, index, mask, width):
    devices, rows, bins = y.shape
    radix, _, quarter, _ = table.shape
    return pl.pallas_call(
        azimuth_kernel,
        grid=(bins // width,),
        in_specs=[
            pl.BlockSpec(table.shape, lambda c: (0, 0, 0, 0)),
            pl.BlockSpec(back.shape, lambda c: (0, 0, 0, 0)),
            pl.BlockSpec((devices, rows, width), lambda c: (0, 0, c)),
            pl.BlockSpec(spectra.shape, lambda c: (0, 0, 0, 0)),
            pl.BlockSpec((1, width), lambda c: (0, c)),
            pl.BlockSpec(mask.shape, lambda c: (0, 0, 0)),
        ],
        out_specs=(
            pl.BlockSpec((2, radix, quarter, width), lambda c: (0, 0, 0, c)),
            pl.BlockSpec((mask.shape[1], width), lambda c: (0, c)),
        ),
        out_shape=(
            jax.ShapeDtypeStruct((2, radix, quarter, bins), BF),
            jax.ShapeDtypeStruct((mask.shape[1], bins), F32),
        ),
        compiler_params=pltpu.CompilerParams(vmem_limit_bytes=48 * 2**20),
        name="azimuth",
    )(table, back, y, spectra, index, mask)


def dft_tables(length, radix):
    quarter = length // radix
    freq = np.arange(quarter, dtype=np.int64)
    tables = []
    for j in range(radix):
        pulse = radix * np.arange(quarter, dtype=np.int64) + j
        angles = (np.outer(freq, pulse) % length) * (2.0 * np.pi / length)
        tables.append(np.stack([np.cos(angles), np.sin(angles)]))
    table = np.stack(tables)
    return jnp.asarray(table, dtype=BF), jnp.asarray(table.swapaxes(2, 3), dtype=BF)


def window_columns(positions, starts, stops):
    inside = (positions[:, None] >= starts[None, :]) & (positions[:, None] < stops[None, :])
    return inside.astype(F32)


def per_device(
    echoes, range_replica, azimuth_replicas, replica_index, azimuth_extent, range_extent
):
    devices = lax.axis_size("row")
    local_pulses, _, samples = echoes.shape
    taps = range_replica.shape[1]
    pulses = local_pulses * devices
    range_bins = samples // devices
    width = 256 if range_bins % 256 == 0 else 128
    radix = 4 if local_pulses % 64 == 0 else 1
    quarter = pulses // radix

    bands = toeplitz(range_replica, width)
    rows = echoes.reshape(local_pulses // radix, radix, 2, samples).transpose(2, 1, 0, 3)
    rows = jnp.pad(rows.reshape(2 * local_pulses, samples), ((0, 0), (0, taps)))
    table, back = dft_tables(pulses, radix)
    replicas, _, azimuth_taps = azimuth_replicas.shape
    split = azimuth_replicas.reshape(replicas, 2, azimuth_taps // radix, radix)
    spectra = pl.pallas_call(
        spectra_kernel,
        out_shape=jax.ShapeDtypeStruct((2, radix, quarter, 2 * replicas), BF),
        compiler_params=pltpu.CompilerParams(vmem_limit_bytes=48 * 2**20),
        name="spectra",
    )(table, split.transpose(1, 3, 2, 0))

    tile_rows = pulses // TILE
    pulse_start = jnp.arange(tile_rows, dtype=jnp.int32) * TILE - azimuth_extent
    pulse_stop = pulse_start + TILE + 2 * azimuth_extent
    order = jnp.arange(radix, dtype=jnp.int32)[:, None, None] + radix * jnp.arange(
        quarter, dtype=jnp.int32
    )
    pulse_mask = (order >= pulse_start[:, None]) & (order < pulse_stop[:, None])
    pulse_count = (jnp.minimum(pulse_stop, pulses) - jnp.maximum(pulse_start, 0)).astype(F32)
    pulse_mask = pulse_mask.astype(BF)

    turned = exchange(rows, bands, devices, range_bins)
    index = replica_index.reshape(1, range_bins)
    image, sums = azimuth(table, back, turned, spectra, index, pulse_mask, width)
    focused = image.transpose(2, 1, 0, 3).reshape(pulses, 2, range_bins)
    ends = devices - 1
    before = lax.ppermute(sums[:, range_bins - EXT :], "row", [(i, i + 1) for i in range(ends)])
    after = lax.ppermute(sums[:, :EXT], "row", [(i + 1, i) for i in range(ends)])
    row_sums = jnp.concatenate([before, sums, after], axis=1)

    local_tiles = range_bins // TILE
    device = lax.axis_index("row")
    tile_ids = device * local_tiles + jnp.arange(local_tiles, dtype=jnp.int32)
    local_extent = lax.dynamic_slice_in_dim(range_extent, device * local_tiles, local_tiles)
    range_start = tile_ids * TILE - local_extent
    range_stop = range_start + TILE + 2 * local_extent
    range_count = (
        jnp.minimum(range_stop, samples) - jnp.maximum(range_start, 0)
    ).astype(F32)
    positions = device * range_bins - EXT + jnp.arange(range_bins + 2 * EXT, dtype=jnp.int32)
    range_mask = window_columns(positions, range_start, range_stop)
    window_sums = jnp.einsum(
        "ct,ic->ti", range_mask, row_sums, precision=HIGHEST, preferred_element_type=F32
    )
    looked = window_sums / (range_count[:, None] * pulse_count[None, :])
    return (focused, looked)


def solution(mesh):
    return jax.shard_map(
        per_device,
        mesh=mesh,
        in_specs=(
            P(("scene", "row"), None, None),
            P(),
            P(),
            P(("scene", "row")),
            P("scene"),
            P("scene"),
        ),
        out_specs=(P("scene", None, "row"), P(("scene", "row"), None)),
        check_vma=False,
    )
```

```python
import functools

import jax
import jax.numpy as jnp
import numpy as np
from jax import lax
from jax.experimental import pallas as pl
from jax.experimental.pallas import tpu as pltpu
from jax.sharding import PartitionSpec as P

TILE = 16
EXT = 16
LANES = 128
HIGHEST = lax.Precision.HIGHEST
BF = jnp.bfloat16
F32 = jnp.float32


def mxu(left, right):
    return jnp.dot(left, right, preferred_element_type=F32)


def block(x_ref, t_ref, offsets):
    rows = x_ref.shape[0]
    half = rows // 2
    depth = t_ref.shape[0]
    width = t_ref.shape[1] // 2
    windows = [x_ref[:, pl.ds(offset, depth)] for offset in offsets]
    result = mxu(jnp.concatenate(windows, axis=0), t_ref[...])
    result = result.reshape(len(offsets), rows, 2 * width)
    real = result[:, :half, :width] + result[:, half:, width:]
    imag = result[:, half:, :width] - result[:, :half, width:]
    return jnp.concatenate([real, imag], axis=1).astype(BF)


def butterfly(parts, sign):
    radix = len(parts)
    if radix == 1:
        return parts
    (ar, ai), (br, bi), (cr, ci), (dr, di) = parts
    pr, pi, qr, qi = ar + cr, ai + ci, ar - cr, ai - ci
    tr, ti, ur, ui = br + dr, bi + di, br - dr, bi - di
    return [
        (pr + tr, pi + ti),
        (qr - sign * ui, qi + sign * ur),
        (pr - tr, pi - ti),
        (qr + sign * ui, qi - sign * ur),
    ]


def forward(table_ref, subsets, length):
    parts = []
    for j, (yr, yi) in enumerate(subsets):
        c, s = table_ref[j, 0, :, :length], table_ref[j, 1, :, :length]
        parts.append((mxu(c, yr) + mxu(s, yi), mxu(c, yi) - mxu(s, yr)))
    return butterfly(parts, -1.0)


def replica_spectra(table_ref, g_ref, out_ref):
    radix, length = g_ref.shape[1], g_ref.shape[2]
    subsets = [(g_ref[0, j], g_ref[1, j]) for j in range(radix)]
    for m, pair in enumerate(forward(table_ref, subsets, length)):
        for part, value in enumerate(pair):
            high = value.astype(BF)
            low = (value - high.astype(F32)).astype(BF)
            out_ref[part, m] = jnp.concatenate([high, low], axis=1)


def azimuth(table_ref, back_ref, y_ref, g_ref, index, mask_ref, out_ref, sums_ref, blocks):
    devices, rows, width = y_ref.shape
    radix, _, quarter, _ = table_ref.shape
    piece = rows // (2 * radix)

    def store(ref, value):
        for i, number in enumerate(blocks):
            ref[:, number * LANES : (number + 1) * LANES] = value[:, i * LANES : (i + 1) * LANES]

    def subset(k):
        return y_ref[:, k * piece : (k + 1) * piece, :].reshape(quarter, width)

    spectrum = forward(table_ref, [(subset(j), subset(radix + j)) for j in range(radix)], quarter)
    replicas = g_ref.shape[3] // 2
    which = lax.rem(lax.broadcasted_iota(jnp.int32, (2 * replicas, width), 0), replicas)
    pick = (which == index).astype(BF)
    scale = 1.0 / (radix * quarter)
    product = []
    for m, (fr, fi) in enumerate(spectrum):
        gr = mxu(g_ref[0, m], pick) * scale
        gi = mxu(g_ref[1, m], pick) * scale
        product.append((fr * gr + fi * gi, fi * gr - fr * gi))
    sums = jnp.zeros((sums_ref.shape[0], width), F32)
    for j, (zr, zi) in enumerate(butterfly(product, 1.0)):
        zr, zi = zr.astype(BF), zi.astype(BF)
        c, s = back_ref[j, 0], back_ref[j, 1]
        ar = mxu(c, zr) - mxu(s, zi)
        ai = mxu(c, zi) + mxu(s, zr)
        store(out_ref.at[0, j], ar.astype(BF))
        store(out_ref.at[1, j], ai.astype(BF))
        power = ar * ar + ai * ai
        high = power.astype(BF)
        low = (power - high.astype(F32)).astype(BF)
        mask = mask_ref[j]
        sums = sums + mxu(mask, high) + mxu(mask, low)
    store(sums_ref, sums)


def focus_kernel(
    devices, bins, chunks,
    x_ref, taps_ref, g_ref, index_ref, mask_ref, table_hbm, back_hbm,
    out_ref, sums_ref, halo_ref,
    bands, packed, turned, table, back, spectra, edges, landed,
    send_sems, recv_sems, edge_send, edge_recv, table_sems,
):
    me = lax.axis_index("row")
    barrier = pltpu.get_barrier_semaphore()
    last = bins // LANES - 1
    loads = [
        pltpu.make_async_copy(table_hbm, table, table_sems.at[0]),
        pltpu.make_async_copy(back_hbm, back, table_sems.at[1]),
    ]
    for load in loads:
        load.start()

    def greet(i, carry):
        pl.semaphore_signal(
            barrier,
            inc=1,
            device_id={"row": lax.rem(me + i, devices)},
            device_id_type=pl.DeviceIdType.MESH,
        )
        return carry

    lax.fori_loop(1, devices, greet, 0)

    for part in range(2):
        taps = taps_ref[part : part + 1, :].astype(F32)
        taps = jnp.concatenate([taps, jnp.zeros((1, LANES), F32)], axis=1)
        taps = jnp.broadcast_to(taps, (LANES, taps.shape[1]))
        band = pltpu.roll(taps, 0, 1, stride=1, stride_axis=0)
        bands[:, part * LANES : (part + 1) * LANES] = band.T.astype(BF)

    def piece(q, target):
        offsets = [pl.multiple_of(target * bins + b * LANES, LANES) for b in chunks[q]]
        result = block(x_ref, bands, offsets)
        return jnp.concatenate([result[i] for i in range(len(offsets))], axis=1)

    def shift_of(t):
        return devices // 2 + (t + 1) // 2 * (1 - 2 * (t % 2))

    def remote(q, t):
        shift = shift_of(t)
        target = lax.rem(me + shift, devices)
        return pltpu.make_async_remote_copy(
            src_ref=packed.at[q, target],
            dst_ref=turned.at[q, me],
            send_sem=send_sems.at[q, shift],
            recv_sem=recv_sems.at[q, shift],
            device_id={"row": target},
            device_id_type=pl.DeviceIdType.MESH,
        )

    def edge(side):
        target = lax.rem(me + (devices - 1 if side == 0 else 1), devices)
        return pltpu.make_async_remote_copy(
            src_ref=edges.at[side],
            dst_ref=landed.at[1 - side],
            send_sem=edge_send.at[side],
            recv_sem=edge_recv.at[side],
            device_id={"row": target},
            device_id_type=pl.DeviceIdType.MESH,
        )

    for q in range(len(chunks)):
        def fill(t, carry, q=q):
            target = lax.rem(me + shift_of(t), devices)
            packed[q, target] = piece(q, target)
            if q > 0:
                remote(q, t).start()
            else:
                @pl.when(t == 0)
                def _():
                    pl.semaphore_wait(barrier, devices - 1)
                remote(q, t).start()
            return carry

        lax.fori_loop(0, devices - 1, fill, 0)
    for q in range(len(chunks)):
        turned[q, me] = piece(q, me)
    for load in loads:
        load.wait()
    replica_spectra(table, g_ref, spectra)

    for q, blocks in enumerate(chunks):
        def finish(t, carry, q=q):
            remote(q, t).wait()
            return carry

        lax.fori_loop(0, devices - 1, finish, 0)
        index = jnp.concatenate(
            [index_ref[:, b * LANES : (b + 1) * LANES] for b in blocks], axis=1
        )
        azimuth(
            table, back, turned.at[q], spectra, index, mask_ref, out_ref, sums_ref, blocks
        )
        for side, number in ((0, 0), (1, last)):
            if number in blocks:
                edges[side] = sums_ref[:, number * LANES : (number + 1) * LANES]
                edge(side).start()
    for side in (0, 1):
        edge(side).wait()
    halo_ref[...] = landed[...]


def focus(x, taps, g, index, mask, table, back, devices, bins):
    rows = x.shape[0]
    radix, _, quarter, _ = table.shape
    tiles = mask.shape[1]
    count = bins // LANES
    if count % 2:
        chunks = [(b,) for b in range(count)]
    else:
        chunks = [(b, count - 1 - b) for b in range(count // 2)]
    width = len(chunks[0]) * LANES
    vmem = pl.BlockSpec(memory_space=pltpu.VMEM)
    anywhere = pl.BlockSpec(memory_space=pl.ANY)
    pieces = pltpu.VMEM((len(chunks), devices, rows, width), BF)
    return pl.pallas_call(
        functools.partial(focus_kernel, devices, bins, chunks),
        in_specs=[vmem] * 5 + [anywhere] * 2,
        out_specs=(vmem, vmem, vmem),
        out_shape=(
            jax.ShapeDtypeStruct((2, radix, quarter, bins), BF),
            jax.ShapeDtypeStruct((tiles, bins), F32),
            jax.ShapeDtypeStruct((2, tiles, LANES), F32),
        ),
        scratch_shapes=[
            pltpu.VMEM((taps.shape[1] + LANES, 2 * LANES), BF),
            pieces,
            pieces,
            pltpu.VMEM(table.shape, BF),
            pltpu.VMEM(back.shape, BF),
            pltpu.VMEM((2, radix, quarter, 2 * g.shape[3]), BF),
            pltpu.VMEM((2, tiles, LANES), F32),
            pltpu.VMEM((2, tiles, LANES), F32),
            pltpu.SemaphoreType.DMA((len(chunks), devices)),
            pltpu.SemaphoreType.DMA((len(chunks), devices)),
            pltpu.SemaphoreType.DMA((2,)),
            pltpu.SemaphoreType.DMA((2,)),
            pltpu.SemaphoreType.DMA((2,)),
        ],
        compiler_params=pltpu.CompilerParams(
            collective_id=0, has_side_effects=True, vmem_limit_bytes=50 * 2**20
        ),
        name="focus",
    )(x, taps, g, index, mask, table, back)


def dft_tables(length, radix):
    quarter = length // radix
    freq = np.arange(quarter, dtype=np.int64)
    tables = []
    for j in range(radix):
        pulse = radix * np.arange(quarter, dtype=np.int64) + j
        angles = (np.outer(freq, pulse) % length) * (2.0 * np.pi / length)
        tables.append(np.stack([np.cos(angles), np.sin(angles)]))
    table = np.stack(tables)
    return jnp.asarray(table, dtype=BF), jnp.asarray(table.swapaxes(2, 3), dtype=BF)


def window_columns(positions, starts, stops):
    inside = (positions[:, None] >= starts[None, :]) & (positions[:, None] < stops[None, :])
    return inside.astype(F32)


def per_device(
    echoes, range_replica, azimuth_replicas, replica_index, azimuth_extent, range_extent
):
    devices = lax.axis_size("row")
    local_pulses, _, samples = echoes.shape
    taps = range_replica.shape[1]
    pulses = local_pulses * devices
    range_bins = samples // devices
    radix = 4 if local_pulses % 64 == 0 else 1
    quarter = pulses // radix

    rows = echoes.reshape(local_pulses // radix, radix, 2, samples).transpose(2, 1, 0, 3)
    rows = jnp.pad(rows.reshape(2 * local_pulses, samples), ((0, 0), (0, taps)))
    table, back = dft_tables(pulses, radix)
    replicas, _, azimuth_taps = azimuth_replicas.shape
    split = azimuth_replicas.reshape(replicas, 2, azimuth_taps // radix, radix)
    tile_rows = pulses // TILE
    pulse_start = jnp.arange(tile_rows, dtype=jnp.int32) * TILE - azimuth_extent
    pulse_stop = pulse_start + TILE + 2 * azimuth_extent
    order = jnp.arange(radix, dtype=jnp.int32)[:, None, None] + radix * jnp.arange(
        quarter, dtype=jnp.int32
    )
    pulse_mask = (order >= pulse_start[:, None]) & (order < pulse_stop[:, None])
    pulse_count = (jnp.minimum(pulse_stop, pulses) - jnp.maximum(pulse_start, 0)).astype(F32)
    pulse_mask = pulse_mask.astype(BF)

    index = replica_index.reshape(1, range_bins)
    image, sums, halo = focus(
        rows, range_replica, split.transpose(1, 3, 2, 0), index, pulse_mask, table, back,
        devices, range_bins,
    )
    focused = image.transpose(2, 1, 0, 3).reshape(pulses, 2, range_bins)
    before, after = halo[0, :, LANES - EXT :], halo[1, :, :EXT]
    row_sums = jnp.concatenate([before, sums, after], axis=1)

    local_tiles = range_bins // TILE
    device = lax.axis_index("row")
    tile_ids = device * local_tiles + jnp.arange(local_tiles, dtype=jnp.int32)
    local_extent = lax.dynamic_slice_in_dim(range_extent, device * local_tiles, local_tiles)
    range_start = tile_ids * TILE - local_extent
    range_stop = range_start + TILE + 2 * local_extent
    range_count = (
        jnp.minimum(range_stop, samples) - jnp.maximum(range_start, 0)
    ).astype(F32)
    positions = device * range_bins - EXT + jnp.arange(range_bins + 2 * EXT, dtype=jnp.int32)
    range_mask = window_columns(
        positions, jnp.maximum(range_start, 0), jnp.minimum(range_stop, samples)
    )
    window_sums = jnp.einsum(
        "ct,ic->ti", range_mask, row_sums, precision=HIGHEST, preferred_element_type=F32
    )
    looked = window_sums / (range_count[:, None] * pulse_count[None, :])
    return (focused, looked)


def solution(mesh):
    return jax.shard_map(
        per_device,
        mesh=mesh,
        in_specs=(
            P(("scene", "row"), None, None),
            P(),
            P(),
            P(("scene", "row")),
            P("scene"),
            P("scene"),
        ),
        out_specs=(P("scene", None, "row"), P(("scene", "row"), None)),
        check_vma=False,
    )
```

```python
import functools

import jax
import jax.numpy as jnp
import numpy as np
from jax import lax
from jax.experimental import pallas as pl
from jax.experimental.pallas import tpu as pltpu
from jax.sharding import PartitionSpec as P

TILE = 16
EXT = 16
LANES = 128
HIGHEST = lax.Precision.HIGHEST
BF = jnp.bfloat16
F32 = jnp.float32


def mxu(left, right):
    return jnp.dot(left, right, preferred_element_type=F32)


def block(x_ref, t_ref, offsets):
    rows = x_ref.shape[0]
    half = rows // 2
    depth = t_ref.shape[0]
    width = t_ref.shape[1] // 2
    windows = [x_ref[:, pl.ds(offset, depth)] for offset in offsets]
    result = mxu(jnp.concatenate(windows, axis=0), t_ref[...])
    result = result.reshape(len(offsets), rows, 2 * width)
    real = result[:, :half, :width] + result[:, half:, width:]
    imag = result[:, half:, :width] - result[:, :half, width:]
    return jnp.concatenate([real, imag], axis=1).astype(BF)


def butterfly(parts, sign):
    radix = len(parts)
    if radix == 1:
        return parts
    (ar, ai), (br, bi), (cr, ci), (dr, di) = parts
    pr, pi, qr, qi = ar + cr, ai + ci, ar - cr, ai - ci
    tr, ti, ur, ui = br + dr, bi + di, br - dr, bi - di
    return [
        (pr + tr, pi + ti),
        (qr - sign * ui, qi + sign * ur),
        (pr - tr, pi - ti),
        (qr + sign * ui, qi - sign * ur),
    ]


def forward(table_ref, subsets, length):
    parts = []
    for j, (yr, yi) in enumerate(subsets):
        c, s = table_ref[j, 0, :, :length], table_ref[j, 1, :, :length]
        parts.append((mxu(c, yr) + mxu(s, yi), mxu(c, yi) - mxu(s, yr)))
    return butterfly(parts, -1.0)


def replica_spectra(table_ref, g_ref, out_ref):
    radix, length = g_ref.shape[1], g_ref.shape[2]
    subsets = [(g_ref[0, j], g_ref[1, j]) for j in range(radix)]
    for m, pair in enumerate(forward(table_ref, subsets, length)):
        for part, value in enumerate(pair):
            high = value.astype(BF)
            low = (value - high.astype(F32)).astype(BF)
            out_ref[part, m] = jnp.concatenate([high, low], axis=1)


def azimuth(table_ref, back_ref, y_ref, g_ref, index, mask_ref, out_ref, sums_ref, blocks):
    devices, rows, width = y_ref.shape
    radix, _, quarter, _ = table_ref.shape
    piece = rows // (2 * radix)

    def store(ref, value):
        for i, number in enumerate(blocks):
            ref[:, number * LANES : (number + 1) * LANES] = value[:, i * LANES : (i + 1) * LANES]

    def subset(k):
        return y_ref[:, k * piece : (k + 1) * piece, :].reshape(quarter, width)

    spectrum = forward(table_ref, [(subset(j), subset(radix + j)) for j in range(radix)], quarter)
    replicas = g_ref.shape[3] // 2
    which = lax.rem(lax.broadcasted_iota(jnp.int32, (2 * replicas, width), 0), replicas)
    pick = (which == index).astype(BF)
    scale = 1.0 / (radix * quarter)
    product = []
    for m, (fr, fi) in enumerate(spectrum):
        gr = mxu(g_ref[0, m], pick) * scale
        gi = mxu(g_ref[1, m], pick) * scale
        product.append((fr * gr + fi * gi, fi * gr - fr * gi))
    sums = jnp.zeros((sums_ref.shape[0], width), F32)
    for j, (zr, zi) in enumerate(butterfly(product, 1.0)):
        zr, zi = zr.astype(BF), zi.astype(BF)
        c, s = back_ref[j, 0], back_ref[j, 1]
        ar = mxu(c, zr) - mxu(s, zi)
        ai = mxu(c, zi) + mxu(s, zr)
        store(out_ref.at[0, j], ar.astype(BF))
        store(out_ref.at[1, j], ai.astype(BF))
        power = ar * ar + ai * ai
        high = power.astype(BF)
        low = (power - high.astype(F32)).astype(BF)
        mask = mask_ref[j]
        sums = sums + mxu(mask, high) + mxu(mask, low)
    store(sums_ref, sums)


def focus_kernel(
    devices, bins, chunks,
    x_hbm, taps_ref, g_ref, index_ref, mask_ref, table_hbm, back_hbm,
    out_ref, sums_ref, halo_ref,
    x_ref, bands, packed, turned, table, back, spectra, edges, landed,
    send_sems, recv_sems, edge_send, edge_recv, table_sems,
):
    me = lax.axis_index("row")
    barrier = pltpu.get_barrier_semaphore()
    last = bins // LANES - 1
    loads = [
        pltpu.make_async_copy(table_hbm, table, table_sems.at[0]),
        pltpu.make_async_copy(back_hbm, back, table_sems.at[1]),
    ]
    samples = x_hbm.shape[1]
    echoes = pltpu.make_async_copy(x_hbm, x_ref.at[:, :samples], table_sems.at[2])
    echoes.start()
    for load in loads:
        load.start()
    x_ref[:, samples:] = jnp.zeros((x_ref.shape[0], x_ref.shape[1] - samples), BF)

    def greet(i, carry):
        pl.semaphore_signal(
            barrier,
            inc=1,
            device_id={"row": lax.rem(me + i, devices)},
            device_id_type=pl.DeviceIdType.MESH,
        )
        return carry

    lax.fori_loop(1, devices, greet, 0)

    for part in range(2):
        taps = taps_ref[part : part + 1, :].astype(F32)
        taps = jnp.concatenate([taps, jnp.zeros((1, LANES), F32)], axis=1)
        taps = jnp.broadcast_to(taps, (LANES, taps.shape[1]))
        band = pltpu.roll(taps, 0, 1, stride=1, stride_axis=0)
        bands[:, part * LANES : (part + 1) * LANES] = band.T.astype(BF)

    echoes.wait()

    def piece(q, target):
        offsets = [pl.multiple_of(target * bins + b * LANES, LANES) for b in chunks[q]]
        result = block(x_ref, bands, offsets)
        return jnp.concatenate([result[i] for i in range(len(offsets))], axis=1)

    def shift_of(t):
        return devices // 2 + (t + 1) // 2 * (1 - 2 * (t % 2))

    def remote(q, t):
        shift = shift_of(t)
        target = lax.rem(me + shift, devices)
        return pltpu.make_async_remote_copy(
            src_ref=packed.at[q, target],
            dst_ref=turned.at[q, me],
            send_sem=send_sems.at[q, shift],
            recv_sem=recv_sems.at[q, shift],
            device_id={"row": target},
            device_id_type=pl.DeviceIdType.MESH,
        )

    def edge(side):
        target = lax.rem(me + (devices - 1 if side == 0 else 1), devices)
        return pltpu.make_async_remote_copy(
            src_ref=edges.at[side],
            dst_ref=landed.at[1 - side],
            send_sem=edge_send.at[side],
            recv_sem=edge_recv.at[side],
            device_id={"row": target},
            device_id_type=pl.DeviceIdType.MESH,
        )

    for q in range(len(chunks)):
        def fill(t, carry, q=q):
            target = lax.rem(me + shift_of(t), devices)
            packed[q, target] = piece(q, target)
            if q > 0:
                remote(q, t).start()
            else:
                @pl.when(t == 0)
                def _():
                    pl.semaphore_wait(barrier, devices - 1)
                remote(q, t).start()
            return carry

        lax.fori_loop(0, devices - 1, fill, 0)
    for q in range(len(chunks)):
        turned[q, me] = piece(q, me)
    for load in loads:
        load.wait()
    replica_spectra(table, g_ref, spectra)

    for q, blocks in enumerate(chunks):
        def finish(t, carry, q=q):
            remote(q, t).wait()
            return carry

        lax.fori_loop(0, devices - 1, finish, 0)
        index = jnp.concatenate(
            [index_ref[:, b * LANES : (b + 1) * LANES] for b in blocks], axis=1
        )
        azimuth(
            table, back, turned.at[q], spectra, index, mask_ref, out_ref, sums_ref, blocks
        )
        for side, number in ((0, 0), (1, last)):
            if number in blocks:
                edges[side] = sums_ref[:, number * LANES : (number + 1) * LANES]
                edge(side).start()
    for side in (0, 1):
        edge(side).wait()
    halo_ref[...] = landed[...]


def focus(x, taps, g, index, mask, table, back, devices, bins):
    rows = x.shape[0]
    radix, _, quarter, _ = table.shape
    tiles = mask.shape[1]
    count = bins // LANES
    if count % 2:
        chunks = [(b,) for b in range(count)]
    else:
        chunks = [(b, count - 1 - b) for b in range(count // 2)]
    width = len(chunks[0]) * LANES
    vmem = pl.BlockSpec(memory_space=pltpu.VMEM)
    anywhere = pl.BlockSpec(memory_space=pl.ANY)
    pieces = pltpu.VMEM((len(chunks), devices, rows, width), BF)
    return pl.pallas_call(
        functools.partial(focus_kernel, devices, bins, chunks),
        in_specs=[anywhere] + [vmem] * 4 + [anywhere] * 2,
        out_specs=(vmem, vmem, vmem),
        out_shape=(
            jax.ShapeDtypeStruct((2, radix, quarter, bins), BF),
            jax.ShapeDtypeStruct((tiles, bins), F32),
            jax.ShapeDtypeStruct((2, tiles, LANES), F32),
        ),
        scratch_shapes=[
            pltpu.VMEM((rows, x.shape[1] + taps.shape[1]), BF),
            pltpu.VMEM((taps.shape[1] + LANES, 2 * LANES), BF),
            pieces,
            pieces,
            pltpu.VMEM(table.shape, BF),
            pltpu.VMEM(back.shape, BF),
            pltpu.VMEM((2, radix, quarter, 2 * g.shape[3]), BF),
            pltpu.VMEM((2, tiles, LANES), F32),
            pltpu.VMEM((2, tiles, LANES), F32),
            pltpu.SemaphoreType.DMA((len(chunks), devices)),
            pltpu.SemaphoreType.DMA((len(chunks), devices)),
            pltpu.SemaphoreType.DMA((2,)),
            pltpu.SemaphoreType.DMA((2,)),
            pltpu.SemaphoreType.DMA((3,)),
        ],
        compiler_params=pltpu.CompilerParams(
            collective_id=0, has_side_effects=True, vmem_limit_bytes=28 * 2**20
        ),
        name="focus",
    )(x, taps, g, index, mask, table, back)


def dft_tables(length, radix):
    quarter = length // radix
    freq = np.arange(quarter, dtype=np.int64)
    tables = []
    for j in range(radix):
        pulse = radix * np.arange(quarter, dtype=np.int64) + j
        angles = (np.outer(freq, pulse) % length) * (2.0 * np.pi / length)
        tables.append(np.stack([np.cos(angles), np.sin(angles)]))
    table = np.stack(tables)
    return jnp.asarray(table, dtype=BF), jnp.asarray(table.swapaxes(2, 3), dtype=BF)


def window_columns(positions, starts, stops):
    inside = (positions[:, None] >= starts[None, :]) & (positions[:, None] < stops[None, :])
    return inside.astype(F32)


def per_device(
    echoes, range_replica, azimuth_replicas, replica_index, azimuth_extent, range_extent
):
    devices = lax.axis_size("row")
    local_pulses, _, samples = echoes.shape
    pulses = local_pulses * devices
    range_bins = samples // devices
    radix = 4 if local_pulses % 64 == 0 else 1
    quarter = pulses // radix

    rows = echoes.reshape(local_pulses // radix, radix, 2, samples).transpose(2, 1, 0, 3)
    rows = rows.reshape(2 * local_pulses, samples)
    table, back = dft_tables(pulses, radix)
    replicas, _, azimuth_taps = azimuth_replicas.shape
    split = azimuth_replicas.reshape(replicas, 2, azimuth_taps // radix, radix)
    tile_rows = pulses // TILE
    pulse_start = jnp.arange(tile_rows, dtype=jnp.int32) * TILE - azimuth_extent
    pulse_stop = pulse_start + TILE + 2 * azimuth_extent
    order = jnp.arange(radix, dtype=jnp.int32)[:, None, None] + radix * jnp.arange(
        quarter, dtype=jnp.int32
    )
    pulse_mask = (order >= pulse_start[:, None]) & (order < pulse_stop[:, None])
    pulse_count = (jnp.minimum(pulse_stop, pulses) - jnp.maximum(pulse_start, 0)).astype(F32)
    pulse_mask = pulse_mask.astype(BF)

    index = replica_index.reshape(1, range_bins)
    image, sums, halo = focus(
        rows, range_replica, split.transpose(1, 3, 2, 0), index, pulse_mask, table, back,
        devices, range_bins,
    )
    focused = image.transpose(2, 1, 0, 3).reshape(pulses, 2, range_bins)
    before, after = halo[0, :, LANES - EXT :], halo[1, :, :EXT]
    row_sums = jnp.concatenate([before, sums, after], axis=1)

    local_tiles = range_bins // TILE
    device = lax.axis_index("row")
    tile_ids = device * local_tiles + jnp.arange(local_tiles, dtype=jnp.int32)
    local_extent = lax.dynamic_slice_in_dim(range_extent, device * local_tiles, local_tiles)
    range_start = tile_ids * TILE - local_extent
    range_stop = range_start + TILE + 2 * local_extent
    range_count = (
        jnp.minimum(range_stop, samples) - jnp.maximum(range_start, 0)
    ).astype(F32)
    positions = device * range_bins - EXT + jnp.arange(range_bins + 2 * EXT, dtype=jnp.int32)
    range_mask = window_columns(
        positions, jnp.maximum(range_start, 0), jnp.minimum(range_stop, samples)
    )
    window_sums = jnp.einsum(
        "ct,ic->ti", range_mask, row_sums, precision=HIGHEST, preferred_element_type=F32
    )
    looked = window_sums / (range_count[:, None] * pulse_count[None, :])
    return (focused, looked)


def solution(mesh):
    return jax.shard_map(
        per_device,
        mesh=mesh,
        in_specs=(
            P(("scene", "row"), None, None),
            P(),
            P(),
            P(("scene", "row")),
            P("scene"),
            P("scene"),
        ),
        out_specs=(P("scene", None, "row"), P(("scene", "row"), None)),
        check_vma=False,
    )
```

```python
import functools

import jax
import jax.numpy as jnp
import numpy as np
from jax import lax
from jax.experimental import pallas as pl
from jax.experimental.pallas import tpu as pltpu
from jax.sharding import PartitionSpec as P

TILE = 16
EXT = 16
LANES = 128
HIGHEST = lax.Precision.HIGHEST
BF = jnp.bfloat16
F32 = jnp.float32


def mxu(left, right):
    return jnp.dot(left, right, preferred_element_type=F32)


def block(x_ref, t_ref, offsets):
    rows = x_ref.shape[0]
    half = rows // 2
    depth = t_ref.shape[0]
    width = t_ref.shape[1] // 2
    windows = [x_ref[:, pl.ds(offset, depth)] for offset in offsets]
    result = mxu(jnp.concatenate(windows, axis=0), t_ref[...])
    result = result.reshape(len(offsets), rows, 2 * width)
    real = result[:, :half, :width] + result[:, half:, width:]
    imag = result[:, half:, :width] - result[:, :half, width:]
    return jnp.concatenate([real, imag], axis=1).astype(BF)


def butterfly(parts, sign):
    radix = len(parts)
    if radix == 1:
        return parts
    (ar, ai), (br, bi), (cr, ci), (dr, di) = parts
    pr, pi, qr, qi = ar + cr, ai + ci, ar - cr, ai - ci
    tr, ti, ur, ui = br + dr, bi + di, br - dr, bi - di
    return [
        (pr + tr, pi + ti),
        (qr - sign * ui, qi + sign * ur),
        (pr - tr, pi - ti),
        (qr + sign * ui, qi - sign * ur),
    ]


def forward(table_ref, subsets, length):
    parts = []
    for j, (yr, yi) in enumerate(subsets):
        c, s = table_ref[j, 0, :, :length], table_ref[j, 1, :, :length]
        parts.append((mxu(c, yr) + mxu(s, yi), mxu(c, yi) - mxu(s, yr)))
    return butterfly(parts, -1.0)


def replica_spectra(table_ref, g_ref, out_ref):
    radix, length = g_ref.shape[1], g_ref.shape[2]
    subsets = [(g_ref[0, j], g_ref[1, j]) for j in range(radix)]
    for m, pair in enumerate(forward(table_ref, subsets, length)):
        for part, value in enumerate(pair):
            high = value.astype(BF)
            low = (value - high.astype(F32)).astype(BF)
            out_ref[part, m] = jnp.concatenate([high, low], axis=1)


def azimuth(table_ref, back_ref, y_ref, g_ref, index, mask_ref, out_ref, sums_ref, blocks):
    devices, rows, width = y_ref.shape
    radix, _, quarter, _ = table_ref.shape
    piece = rows // (2 * radix)

    def store(ref, value):
        for i, number in enumerate(blocks):
            ref[:, number * LANES : (number + 1) * LANES] = value[:, i * LANES : (i + 1) * LANES]

    def subset(k):
        return y_ref[:, k * piece : (k + 1) * piece, :].reshape(quarter, width)

    spectrum = forward(table_ref, [(subset(j), subset(radix + j)) for j in range(radix)], quarter)
    replicas = g_ref.shape[3] // 2
    which = lax.rem(lax.broadcasted_iota(jnp.int32, (2 * replicas, width), 0), replicas)
    pick = (which == index).astype(BF)
    scale = 1.0 / (radix * quarter)
    product = []
    for m, (fr, fi) in enumerate(spectrum):
        gr = mxu(g_ref[0, m], pick) * scale
        gi = mxu(g_ref[1, m], pick) * scale
        product.append((fr * gr + fi * gi, fi * gr - fr * gi))
    sums = jnp.zeros((sums_ref.shape[0], width), F32)
    for j, (zr, zi) in enumerate(butterfly(product, 1.0)):
        zr, zi = zr.astype(BF), zi.astype(BF)
        c, s = back_ref[j, 0], back_ref[j, 1]
        ar = mxu(c, zr) - mxu(s, zi)
        ai = mxu(c, zi) + mxu(s, zr)
        store(out_ref.at[0, j], ar.astype(BF))
        store(out_ref.at[1, j], ai.astype(BF))
        power = ar * ar + ai * ai
        high = power.astype(BF)
        low = (power - high.astype(F32)).astype(BF)
        mask = mask_ref[j]
        sums = sums + mxu(mask, high) + mxu(mask, low)
    store(sums_ref, sums)


def focus_kernel(
    devices, bins, chunks,
    x_hbm, taps_ref, g_ref, index_ref, mask_ref, table_hbm,
    out_ref, sums_ref, halo_ref,
    x_ref, bands, packed, turned, table, back, spectra, edges, landed,
    send_sems, recv_sems, edge_send, edge_recv, table_sems,
):
    me = lax.axis_index("row")
    barrier = pltpu.get_barrier_semaphore()
    last = bins // LANES - 1
    load = pltpu.make_async_copy(table_hbm, table, table_sems.at[0])
    samples = x_hbm.shape[1]
    echoes = pltpu.make_async_copy(x_hbm, x_ref.at[:, :samples], table_sems.at[1])
    echoes.start()
    load.start()
    x_ref[:, samples:] = jnp.zeros((x_ref.shape[0], x_ref.shape[1] - samples), BF)

    def greet(i, carry):
        pl.semaphore_signal(
            barrier,
            inc=1,
            device_id={"row": lax.rem(me + i, devices)},
            device_id_type=pl.DeviceIdType.MESH,
        )
        return carry

    lax.fori_loop(1, devices, greet, 0)

    for part in range(2):
        taps = taps_ref[part : part + 1, :].astype(F32)
        taps = jnp.concatenate([taps, jnp.zeros((1, LANES), F32)], axis=1)
        taps = jnp.broadcast_to(taps, (LANES, taps.shape[1]))
        band = pltpu.roll(taps, 0, 1, stride=1, stride_axis=0)
        bands[:, part * LANES : (part + 1) * LANES] = band.T.astype(BF)

    echoes.wait()

    def piece(q, target):
        offsets = [pl.multiple_of(target * bins + b * LANES, LANES) for b in chunks[q]]
        result = block(x_ref, bands, offsets)
        return jnp.concatenate([result[i] for i in range(len(offsets))], axis=1)

    def shift_of(t):
        return devices // 2 + (t + 1) // 2 * (1 - 2 * (t % 2))

    def remote(q, t):
        shift = shift_of(t)
        target = lax.rem(me + shift, devices)
        return pltpu.make_async_remote_copy(
            src_ref=packed.at[q, target],
            dst_ref=turned.at[q, me],
            send_sem=send_sems.at[q, shift],
            recv_sem=recv_sems.at[q, shift],
            device_id={"row": target},
            device_id_type=pl.DeviceIdType.MESH,
        )

    def edge(side):
        target = lax.rem(me + (devices - 1 if side == 0 else 1), devices)
        return pltpu.make_async_remote_copy(
            src_ref=edges.at[side],
            dst_ref=landed.at[1 - side],
            send_sem=edge_send.at[side],
            recv_sem=edge_recv.at[side],
            device_id={"row": target},
            device_id_type=pl.DeviceIdType.MESH,
        )

    for q in range(len(chunks)):
        def fill(t, carry, q=q):
            target = lax.rem(me + shift_of(t), devices)
            packed[q, target] = piece(q, target)
            if q > 0:
                remote(q, t).start()
            else:
                @pl.when(t == 0)
                def _():
                    pl.semaphore_wait(barrier, devices - 1)
                remote(q, t).start()
            return carry

        lax.fori_loop(0, devices - 1, fill, 0)
    for q in range(len(chunks)):
        turned[q, me] = piece(q, me)
    load.wait()
    for j in range(table.shape[0]):
        for part in range(2):
            back[j, part] = table[j, part].astype(F32).T.astype(BF)
    replica_spectra(table, g_ref, spectra)

    for q, blocks in enumerate(chunks):
        def finish(t, carry, q=q):
            remote(q, t).wait()
            return carry

        lax.fori_loop(0, devices - 1, finish, 0)
        index = jnp.concatenate(
            [index_ref[:, b * LANES : (b + 1) * LANES] for b in blocks], axis=1
        )
        azimuth(
            table, back, turned.at[q], spectra, index, mask_ref, out_ref, sums_ref, blocks
        )
        for side, number in ((0, 0), (1, last)):
            if number in blocks:
                edges[side] = sums_ref[:, number * LANES : (number + 1) * LANES]
                edge(side).start()
    for side in (0, 1):
        edge(side).wait()
    halo_ref[...] = landed[...]


def focus(x, taps, g, index, mask, table, devices, bins):
    rows = x.shape[0]
    radix, _, quarter, _ = table.shape
    tiles = mask.shape[1]
    count = bins // LANES
    if count % 2:
        chunks = [(b,) for b in range(count)]
    else:
        chunks = [(b, count - 1 - b) for b in range(count // 2)]
    width = len(chunks[0]) * LANES
    vmem = pl.BlockSpec(memory_space=pltpu.VMEM)
    anywhere = pl.BlockSpec(memory_space=pl.ANY)
    pieces = pltpu.VMEM((len(chunks), devices, rows, width), BF)
    return pl.pallas_call(
        functools.partial(focus_kernel, devices, bins, chunks),
        in_specs=[anywhere] + [vmem] * 4 + [anywhere],
        out_specs=(vmem, vmem, vmem),
        out_shape=(
            jax.ShapeDtypeStruct((2, radix, quarter, bins), BF),
            jax.ShapeDtypeStruct((tiles, bins), F32),
            jax.ShapeDtypeStruct((2, tiles, LANES), F32),
        ),
        scratch_shapes=[
            pltpu.VMEM((rows, x.shape[1] + taps.shape[1]), BF),
            pltpu.VMEM((taps.shape[1] + LANES, 2 * LANES), BF),
            pieces,
            pieces,
            pltpu.VMEM(table.shape, BF),
            pltpu.VMEM(table.shape, BF),
            pltpu.VMEM((2, radix, quarter, 2 * g.shape[3]), BF),
            pltpu.VMEM((2, tiles, LANES), F32),
            pltpu.VMEM((2, tiles, LANES), F32),
            pltpu.SemaphoreType.DMA((len(chunks), devices)),
            pltpu.SemaphoreType.DMA((len(chunks), devices)),
            pltpu.SemaphoreType.DMA((2,)),
            pltpu.SemaphoreType.DMA((2,)),
            pltpu.SemaphoreType.DMA((2,)),
        ],
        compiler_params=pltpu.CompilerParams(
            collective_id=0, has_side_effects=True, vmem_limit_bytes=28 * 2**20
        ),
        name="focus",
    )(x, taps, g, index, mask, table)


def dft_tables(length, radix):
    quarter = length // radix
    freq = np.arange(quarter, dtype=np.int64)
    tables = []
    for j in range(radix):
        pulse = radix * np.arange(quarter, dtype=np.int64) + j
        angles = (np.outer(freq, pulse) % length) * (2.0 * np.pi / length)
        tables.append(np.stack([np.cos(angles), np.sin(angles)]))
    table = np.stack(tables)
    return jnp.asarray(table, dtype=BF)


def window_columns(positions, starts, stops):
    inside = (positions[:, None] >= starts[None, :]) & (positions[:, None] < stops[None, :])
    return inside.astype(F32)


def per_device(
    echoes, range_replica, azimuth_replicas, replica_index, azimuth_extent, range_extent
):
    devices = lax.axis_size("row")
    local_pulses, _, samples = echoes.shape
    pulses = local_pulses * devices
    range_bins = samples // devices
    radix = 4 if local_pulses % 64 == 0 else 1
    quarter = pulses // radix

    rows = echoes.reshape(local_pulses // radix, radix, 2, samples).transpose(2, 1, 0, 3)
    rows = rows.reshape(2 * local_pulses, samples)
    table = dft_tables(pulses, radix)
    replicas, _, azimuth_taps = azimuth_replicas.shape
    split = azimuth_replicas.reshape(replicas, 2, azimuth_taps // radix, radix)
    tile_rows = pulses // TILE
    pulse_start = jnp.arange(tile_rows, dtype=jnp.int32) * TILE - azimuth_extent
    pulse_stop = pulse_start + TILE + 2 * azimuth_extent
    order = jnp.arange(radix, dtype=jnp.int32)[:, None, None] + radix * jnp.arange(
        quarter, dtype=jnp.int32
    )
    pulse_mask = (order >= pulse_start[:, None]) & (order < pulse_stop[:, None])
    pulse_count = (jnp.minimum(pulse_stop, pulses) - jnp.maximum(pulse_start, 0)).astype(F32)
    pulse_mask = pulse_mask.astype(BF)

    index = replica_index.reshape(1, range_bins)
    image, sums, halo = focus(
        rows, range_replica, split.transpose(1, 3, 2, 0), index, pulse_mask, table,
        devices, range_bins,
    )
    focused = image.transpose(2, 1, 0, 3).reshape(pulses, 2, range_bins)
    before, after = halo[0, :, LANES - EXT :], halo[1, :, :EXT]
    row_sums = jnp.concatenate([before, sums, after], axis=1)

    local_tiles = range_bins // TILE
    device = lax.axis_index("row")
    tile_ids = device * local_tiles + jnp.arange(local_tiles, dtype=jnp.int32)
    local_extent = lax.dynamic_slice_in_dim(range_extent, device * local_tiles, local_tiles)
    range_start = tile_ids * TILE - local_extent
    range_stop = range_start + TILE + 2 * local_extent
    range_count = (
        jnp.minimum(range_stop, samples) - jnp.maximum(range_start, 0)
    ).astype(F32)
    positions = device * range_bins - EXT + jnp.arange(range_bins + 2 * EXT, dtype=jnp.int32)
    range_mask = window_columns(
        positions, jnp.maximum(range_start, 0), jnp.minimum(range_stop, samples)
    )
    window_sums = jnp.einsum(
        "ct,ic->ti", range_mask, row_sums, precision=HIGHEST, preferred_element_type=F32
    )
    looked = window_sums / (range_count[:, None] * pulse_count[None, :])
    return (focused, looked)


def solution(mesh):
    return jax.shard_map(
        per_device,
        mesh=mesh,
        in_specs=(
            P(("scene", "row"), None, None),
            P(),
            P(),
            P(("scene", "row")),
            P("scene"),
            P("scene"),
        ),
        out_specs=(P("scene", None, "row"), P(("scene", "row"), None)),
        check_vma=False,
    )
```

```python
import functools

import jax
import jax.numpy as jnp
import numpy as np
from jax import lax
from jax.experimental import pallas as pl
from jax.experimental.pallas import tpu as pltpu
from jax.sharding import PartitionSpec as P

TILE = 16
EXT = 16
LANES = 128
HIGHEST = lax.Precision.HIGHEST
BF = jnp.bfloat16
F32 = jnp.float32


def mxu(left, right):
    return jnp.dot(left, right, preferred_element_type=F32)


def block(x_ref, t_ref, offsets):
    rows = x_ref.shape[0]
    half = rows // 2
    depth = t_ref.shape[0]
    width = t_ref.shape[1] // 2
    windows = [x_ref[:, pl.ds(offset, depth)] for offset in offsets]
    result = mxu(jnp.concatenate(windows, axis=0), t_ref[...])
    result = result.reshape(len(offsets), rows, 2 * width)
    real = result[:, :half, :width] + result[:, half:, width:]
    imag = result[:, half:, :width] - result[:, :half, width:]
    return jnp.concatenate([real, imag], axis=1).astype(BF)


def butterfly(parts, sign):
    radix = len(parts)
    if radix == 1:
        return parts
    (ar, ai), (br, bi), (cr, ci), (dr, di) = parts
    pr, pi, qr, qi = ar + cr, ai + ci, ar - cr, ai - ci
    tr, ti, ur, ui = br + dr, bi + di, br - dr, bi - di
    return [
        (pr + tr, pi + ti),
        (qr - sign * ui, qi + sign * ur),
        (pr - tr, pi - ti),
        (qr + sign * ui, qi - sign * ur),
    ]


def forward(table_ref, subsets, length):
    parts = []
    for j, (yr, yi) in enumerate(subsets):
        c, s = table_ref[j, 0, :, :length], table_ref[j, 1, :, :length]
        parts.append((mxu(c, yr) + mxu(s, yi), mxu(c, yi) - mxu(s, yr)))
    return butterfly(parts, -1.0)


def replica_spectra(table_ref, g_ref, out_ref):
    radix, length = g_ref.shape[1], g_ref.shape[2]
    subsets = [(g_ref[0, j], g_ref[1, j]) for j in range(radix)]
    for m, pair in enumerate(forward(table_ref, subsets, length)):
        for part, value in enumerate(pair):
            high = value.astype(BF)
            low = (value - high.astype(F32)).astype(BF)
            out_ref[part, m] = jnp.concatenate([high, low], axis=1)


def azimuth(table_ref, back_ref, y_ref, g_ref, index, mask_ref, out_ref, sums_ref, blocks):
    devices, rows, width = y_ref.shape
    radix, _, quarter, _ = table_ref.shape
    piece = rows // (2 * radix)

    def store(ref, value):
        for i, number in enumerate(blocks):
            ref[:, number * LANES : (number + 1) * LANES] = value[:, i * LANES : (i + 1) * LANES]

    def subset(k):
        return y_ref[:, k * piece : (k + 1) * piece, :].reshape(quarter, width)

    spectrum = forward(table_ref, [(subset(j), subset(radix + j)) for j in range(radix)], quarter)
    replicas = g_ref.shape[3] // 2
    which = lax.rem(lax.broadcasted_iota(jnp.int32, (2 * replicas, width), 0), replicas)
    pick = (which == index).astype(BF)
    scale = 1.0 / (radix * quarter)
    product = []
    for m, (fr, fi) in enumerate(spectrum):
        gr = mxu(g_ref[0, m], pick) * scale
        gi = mxu(g_ref[1, m], pick) * scale
        product.append((fr * gr + fi * gi, fi * gr - fr * gi))
    sums = jnp.zeros((sums_ref.shape[0], width), F32)
    for j, (zr, zi) in enumerate(butterfly(product, 1.0)):
        zr, zi = zr.astype(BF), zi.astype(BF)
        c, s = back_ref[j, 0], back_ref[j, 1]
        ar = mxu(c, zr) - mxu(s, zi)
        ai = mxu(c, zi) + mxu(s, zr)
        store(out_ref.at[0, j], ar.astype(BF))
        store(out_ref.at[1, j], ai.astype(BF))
        power = ar * ar + ai * ai
        high = power.astype(BF)
        low = (power - high.astype(F32)).astype(BF)
        mask = mask_ref[j]
        sums = sums + mxu(mask, high) + mxu(mask, low)
    store(sums_ref, sums)


def focus_kernel(
    devices, bins, chunks,
    x_hbm, taps_ref, g_ref, index_ref, mask_ref, table_hbm,
    out_ref, sums_ref, halo_ref,
    x_ref, bands, packed, turned, table, back, spectra, edges, landed,
    send_sems, recv_sems, edge_send, edge_recv, table_sems,
):
    me = lax.axis_index("row")
    barrier = pltpu.get_barrier_semaphore()
    last = bins // LANES - 1
    load = pltpu.make_async_copy(table_hbm, table, table_sems.at[0])
    samples = x_hbm.shape[1]
    echoes = pltpu.make_async_copy(x_hbm, x_ref.at[:, :samples], table_sems.at[1])
    echoes.start()
    load.start()
    x_ref[:, samples:] = jnp.zeros((x_ref.shape[0], x_ref.shape[1] - samples), BF)

    def greet(i, carry):
        pl.semaphore_signal(
            barrier,
            inc=1,
            device_id={"row": lax.rem(me + i, devices)},
            device_id_type=pl.DeviceIdType.MESH,
        )
        return carry

    lax.fori_loop(1, devices, greet, 0)

    for part in range(2):
        taps = taps_ref[part : part + 1, :].astype(F32)
        taps = jnp.concatenate([taps, jnp.zeros((1, LANES), F32)], axis=1)
        taps = jnp.broadcast_to(taps, (LANES, taps.shape[1]))
        band = pltpu.roll(taps, 0, 1, stride=1, stride_axis=0)
        bands[:, part * LANES : (part + 1) * LANES] = band.T.astype(BF)

    echoes.wait()

    def piece(q, target):
        offsets = [pl.multiple_of(target * bins + b * LANES, LANES) for b in chunks[q]]
        result = block(x_ref, bands, offsets)
        return jnp.concatenate([result[i] for i in range(len(offsets))], axis=1)

    def shift_of(t):
        return devices // 2 + (t + 1) // 2 * (1 - 2 * (t % 2))

    def remote(q, t):
        shift = shift_of(t)
        target = lax.rem(me + shift, devices)
        return pltpu.make_async_remote_copy(
            src_ref=packed.at[q, target],
            dst_ref=turned.at[q, me],
            send_sem=send_sems.at[q, shift],
            recv_sem=recv_sems.at[q, shift],
            device_id={"row": target},
            device_id_type=pl.DeviceIdType.MESH,
        )

    def edge(side):
        target = lax.rem(me + (devices - 1 if side == 0 else 1), devices)
        return pltpu.make_async_remote_copy(
            src_ref=edges.at[side],
            dst_ref=landed.at[1 - side],
            send_sem=edge_send.at[side],
            recv_sem=edge_recv.at[side],
            device_id={"row": target},
            device_id_type=pl.DeviceIdType.MESH,
        )

    for q in range(len(chunks)):
        def fill(t, carry, q=q):
            target = lax.rem(me + shift_of(t), devices)
            packed[q, target] = piece(q, target)
            if q > 0:
                remote(q, t).start()
            else:
                @pl.when(t == 0)
                def _():
                    pl.semaphore_wait(barrier, devices - 1)
                remote(q, t).start()
            return carry

        lax.fori_loop(0, devices - 1, fill, 0)
    for q in range(len(chunks)):
        turned[q, me] = piece(q, me)
    load.wait()
    for j in range(table.shape[0]):
        for part in range(2):
            back[j, part] = table[j, part].astype(F32).T.astype(BF)
    replica_spectra(table, g_ref, spectra)

    for q, blocks in enumerate(chunks):
        def finish(t, carry, q=q):
            remote(q, t).wait()
            return carry

        lax.fori_loop(0, devices - 1, finish, 0)
        index = jnp.concatenate(
            [index_ref[:, b * LANES : (b + 1) * LANES] for b in blocks], axis=1
        )
        azimuth(
            table, back, turned.at[q], spectra, index, mask_ref, out_ref, sums_ref, blocks
        )
        for side, number in ((0, 0), (1, last)):
            if number in blocks:
                edges[side] = sums_ref[:, number * LANES : (number + 1) * LANES]
                edge(side).start()
    for side in (0, 1):
        edge(side).wait()
    halo_ref[...] = landed[...]


def focus(x, taps, g, index, mask, table, devices, bins):
    rows = x.shape[0]
    radix, _, quarter, _ = table.shape
    tiles = mask.shape[1]
    count = bins // LANES
    chunks = [(b,) for b in sorted(range(count), key=lambda b: min(b, count - 1 - b))]
    width = len(chunks[0]) * LANES
    vmem = pl.BlockSpec(memory_space=pltpu.VMEM)
    anywhere = pl.BlockSpec(memory_space=pl.ANY)
    pieces = pltpu.VMEM((len(chunks), devices, rows, width), BF)
    return pl.pallas_call(
        functools.partial(focus_kernel, devices, bins, chunks),
        in_specs=[anywhere] + [vmem] * 4 + [anywhere],
        out_specs=(vmem, vmem, vmem),
        out_shape=(
            jax.ShapeDtypeStruct((2, radix, quarter, bins), BF),
            jax.ShapeDtypeStruct((tiles, bins), F32),
            jax.ShapeDtypeStruct((2, tiles, LANES), F32),
        ),
        scratch_shapes=[
            pltpu.VMEM((rows, x.shape[1] + taps.shape[1]), BF),
            pltpu.VMEM((taps.shape[1] + LANES, 2 * LANES), BF),
            pieces,
            pieces,
            pltpu.VMEM(table.shape, BF),
            pltpu.VMEM(table.shape, BF),
            pltpu.VMEM((2, radix, quarter, 2 * g.shape[3]), BF),
            pltpu.VMEM((2, tiles, LANES), F32),
            pltpu.VMEM((2, tiles, LANES), F32),
            pltpu.SemaphoreType.DMA((len(chunks), devices)),
            pltpu.SemaphoreType.DMA((len(chunks), devices)),
            pltpu.SemaphoreType.DMA((2,)),
            pltpu.SemaphoreType.DMA((2,)),
            pltpu.SemaphoreType.DMA((2,)),
        ],
        compiler_params=pltpu.CompilerParams(
            collective_id=0, has_side_effects=True, vmem_limit_bytes=28 * 2**20
        ),
        name="focus",
    )(x, taps, g, index, mask, table)


def dft_tables(length, radix):
    quarter = length // radix
    freq = np.arange(quarter, dtype=np.int64)
    tables = []
    for j in range(radix):
        pulse = radix * np.arange(quarter, dtype=np.int64) + j
        angles = (np.outer(freq, pulse) % length) * (2.0 * np.pi / length)
        tables.append(np.stack([np.cos(angles), np.sin(angles)]))
    table = np.stack(tables)
    return jnp.asarray(table, dtype=BF)


def window_columns(positions, starts, stops):
    inside = (positions[:, None] >= starts[None, :]) & (positions[:, None] < stops[None, :])
    return inside.astype(F32)


def per_device(
    echoes, range_replica, azimuth_replicas, replica_index, azimuth_extent, range_extent
):
    devices = lax.axis_size("row")
    local_pulses, _, samples = echoes.shape
    pulses = local_pulses * devices
    range_bins = samples // devices
    radix = 4 if local_pulses % 64 == 0 else 1
    quarter = pulses // radix

    rows = echoes.reshape(local_pulses // radix, radix, 2, samples).transpose(2, 1, 0, 3)
    rows = rows.reshape(2 * local_pulses, samples)
    table = dft_tables(pulses, radix)
    replicas, _, azimuth_taps = azimuth_replicas.shape
    split = azimuth_replicas.reshape(replicas, 2, azimuth_taps // radix, radix)
    tile_rows = pulses // TILE
    pulse_start = jnp.arange(tile_rows, dtype=jnp.int32) * TILE - azimuth_extent
    pulse_stop = pulse_start + TILE + 2 * azimuth_extent
    order = jnp.arange(radix, dtype=jnp.int32)[:, None, None] + radix * jnp.arange(
        quarter, dtype=jnp.int32
    )
    pulse_mask = (order >= pulse_start[:, None]) & (order < pulse_stop[:, None])
    pulse_count = (jnp.minimum(pulse_stop, pulses) - jnp.maximum(pulse_start, 0)).astype(F32)
    pulse_mask = pulse_mask.astype(BF)

    index = replica_index.reshape(1, range_bins)
    image, sums, halo = focus(
        rows, range_replica, split.transpose(1, 3, 2, 0), index, pulse_mask, table,
        devices, range_bins,
    )
    focused = image.transpose(2, 1, 0, 3).reshape(pulses, 2, range_bins)
    before, after = halo[0, :, LANES - EXT :], halo[1, :, :EXT]
    row_sums = jnp.concatenate([before, sums, after], axis=1)

    local_tiles = range_bins // TILE
    device = lax.axis_index("row")
    tile_ids = device * local_tiles + jnp.arange(local_tiles, dtype=jnp.int32)
    local_extent = lax.dynamic_slice_in_dim(range_extent, device * local_tiles, local_tiles)
    range_start = tile_ids * TILE - local_extent
    range_stop = range_start + TILE + 2 * local_extent
    range_count = (
        jnp.minimum(range_stop, samples) - jnp.maximum(range_start, 0)
    ).astype(F32)
    positions = device * range_bins - EXT + jnp.arange(range_bins + 2 * EXT, dtype=jnp.int32)
    range_mask = window_columns(
        positions, jnp.maximum(range_start, 0), jnp.minimum(range_stop, samples)
    )
    window_sums = jnp.einsum(
        "ct,ic->ti", range_mask, row_sums, precision=HIGHEST, preferred_element_type=F32
    )
    looked = window_sums / (range_count[:, None] * pulse_count[None, :])
    return (focused, looked)


def solution(mesh):
    return jax.shard_map(
        per_device,
        mesh=mesh,
        in_specs=(
            P(("scene", "row"), None, None),
            P(),
            P(),
            P(("scene", "row")),
            P("scene"),
            P("scene"),
        ),
        out_specs=(P("scene", None, "row"), P(("scene", "row"), None)),
        check_vma=False,
    )
```
